32 devices in a mesh: tok: 8 (over z, core), feat: 4 (over y, x).
Axes of the slice: x: 2, y: 2, z: 4, core: 2. Of those that a mesh axis runs over, the one named last changes fastest.
Arguments:
- teacher: float32 [4096, 16384], P('tok', 'feat'), may hold values from -720 to 720, as said below
- student: float32 [4096, 2048], P('tok', 'feat'), may hold values from -6 to 6
- gain: float32 [16384], P('feat'), may hold values from 0.1 to 1.9
- projector: float32 [2048, 16384], P(None, 'feat'), may hold values from -0.1875 to 0.1875
- momentum: float32 [2048, 16384], P('tok', 'feat'), may hold values from -0.12 to 0.12
Outputs:
- new_projector: float32 [2048, 16384], P('tok', 'feat')
- new_momentum: float32 [2048, 16384], P('tok', 'feat')
- student_grad: float32 [4096, 2048], P('tok', 'feat')
- loss_value: float32 [], replicated
The draws below stay inside these ranges and needn't reach their ends.
Inputs may be any that keep to these rules, and one draw needn't show every extreme that they name: `teacher`: finite real values.
All inputs are finite; a program needn't handle non-finite values.
Results may differ from the reference program's by a relative error of at most 0.00011.
Values sent between devices are 32-bit elements; how exact they have to be, the bound alone decides.
A program may use at most 192 MiB of HBM per device.

```python
import math
import jax
import jax.numpy as jnp
from jax import lax

DS = 2048
DT = 16384
TOKENS = 4096


def draw_teacher(key, part):
    key_rows, key_cols, key_noise = jax.random.split(key, 3)
    row_part = jnp.exp(jax.random.uniform(key_rows, (TOKENS, 1), minval=0.0, maxval=math.log(10.0)))
    col_trend = jnp.exp(math.log(3.0) * jnp.arange(DT, dtype=jnp.float32) / DT)
    col_part = col_trend * jnp.exp(jax.random.uniform(key_cols, (DT,), minval=0.0, maxval=math.log(4.0)))
    noise_base = jnp.clip(jax.random.normal(key_noise, (TOKENS, DT)), -6.0, 6.0)
    return (row_part * col_part[None, :] * noise_base).astype(jnp.float32)


def with_spikes(drawn, rng, source, target, shards_of, factor):
    owner, partner = [(jnp.arange(drawn.shape[position]) // (drawn.shape[position] // shards_of)).reshape([-1 if axis == position else 1 for axis in range(drawn.ndim)]) for position in (source, target)]
    chosen = jax.random.permutation(rng, shards_of)[partner]
    strong = (owner == chosen) | (owner == (partner + shards_of // 2) % shards_of)
    return jnp.where(strong, factor * drawn, drawn)


def level_of(rng, extent, shards, smallest, top_value):
    factor_of, own = 1.0, jax.random.fold_in(rng, 6)
    for axis_at, parts in shards:
        heights = jnp.exp(jax.random.uniform(jax.random.fold_in(own, axis_at), (parts,), jnp.float32, smallest / len(shards), top_value / len(shards)))
        factor_of = factor_of * jnp.repeat(heights, extent[axis_at] // parts).reshape([-1 if axis == axis_at else 1 for axis in range(len(extent))])
    return factor_of


def noise(own_key, shape, spread, limit, pieces=(), kind=jnp.bfloat16):
    values = spread * jax.random.normal(own_key, shape, jnp.float32)
    if pieces:
        values = values * level_of(own_key, shape, pieces, -0.22, 0.18)
    return jnp.clip(values, -limit, limit).astype(kind)


def noise_with(rng, extent, deviation, limit, cuts, heavy, kind=jnp.bfloat16):
    array = deviation * jax.random.normal(rng, extent, jnp.float32)
    if cuts:
        array = array * level_of(rng, extent, cuts, -0.22, 0.18)
    return jnp.clip(with_spikes(array, jax.random.fold_in(rng, 3), *heavy), -limit, limit).astype(kind)


def setup_inputs(seed: int = 0) -> dict:
    key_list = jax.random.split(jax.random.key(seed), 6)
    teacher = draw_teacher(jax.random.fold_in(key_list[5], 71), 0)
    student = noise_with(key_list[1], (TOKENS, DS), 1.0, 6.0, ((0, 8), (1, 4)), (0, 1, 8, 2.0), jnp.float32)
    gain = jnp.clip(1.0 + 0.18 * jax.random.normal(key_list[2], (DT,), jnp.float32), 0.1, 1.9)
    projector = noise_with(key_list[3], (DS, DT), DS ** -0.5, 0.1875, ((1, 4),), (1, 0, 4, 2.0), jnp.float32)
    momentum = noise(key_list[4], (DS, DT), 0.02, 0.12, ((0, 8), (1, 4)), jnp.float32)
    return {"teacher": teacher, "student": student, "gain": gain, "projector": projector, "momentum": momentum}


norm_eps = 1e-05
momentum_rate = 0.9
step_rate = 0.5

def reference(teacher, student, gain, projector, momentum):
    highest = lax.Precision.HIGHEST
    row_total = lax.optimization_barrier(jnp.sum(teacher * teacher, axis=1, keepdims=True))
    row_scale = lax.rsqrt(row_total / DT + norm_eps)
    target = teacher * row_scale * gain[None, :]
    predicted = jnp.dot(student, projector, precision=highest, preferred_element_type=jnp.float32)
    residual = predicted - target
    loss_value = jnp.sum(residual * residual) / (TOKENS * DT)
    proj_grad = lax.dot_general(student, residual, (((0,), (0,)), ((), ())), precision=highest, preferred_element_type=jnp.float32) / TOKENS
    student_grad = lax.dot_general(residual, projector, (((1,), (1,)), ((), ())), precision=highest, preferred_element_type=jnp.float32)
    new_momentum = momentum_rate * momentum + proj_grad
    new_projector = projector - step_rate * new_momentum
    return (new_projector, new_momentum, student_grad, loss_value)
```

```python
import jax
import jax.numpy as jnp
from jax import lax
from jax.sharding import PartitionSpec as P

norm_eps = 1e-05
momentum_rate = 0.9
step_rate = 0.5
PIECES = 4


def product(a, b, ca, cb):
    return lax.dot_general(
        a,
        b,
        (((ca,), (cb,)), ((), ())),
        precision=lax.Precision.HIGH,
        preferred_element_type=jnp.float32,
    )


def on_device(teacher, student, gain, projector, momentum):
    rows, cols = teacher.shape
    tok = lax.axis_size("tok")
    feat = lax.axis_size("feat")
    chips = tok // 2
    own = momentum.shape[0]
    me = lax.axis_index("tok")
    chip, core = me // 2, me % 2
    token_count = rows * tok
    width = cols // PIECES
    swap = [(i, i ^ 1) for i in range(tok)]

    full_student = lax.all_gather(student, "feat", axis=1, tiled=True)
    squares = jnp.sum(teacher * teacher, axis=1)
    row_total = lax.psum(squares, "feat")
    row_scale = lax.rsqrt(row_total / (cols * feat) + norm_eps)[:, None]

    def columns_of(index):
        blocks = [
            lax.dynamic_slice_in_dim(full_student, (2 * i + index) * own, own, 1)
            for i in range(chips)
        ]
        return jnp.concatenate(blocks, axis=1)

    mine = columns_of(core)
    other = lax.ppermute(columns_of(1 - core), "tok", swap)

    def pick(terms, index):
        return lax.dynamic_index_in_dim(terms, index, 0, False)

    tie = lax.optimization_barrier
    residuals, swaps, firsts, all_terms, got, done = [], [], [], [], {}, []

    def predict(p, after):
        part = slice(p * width, (p + 1) * width)
        states = tie((full_student, after))[0]
        predicted = product(states, projector[:, part], 1, 0)
        residual = predicted - teacher[:, part] * row_scale * gain[None, part]
        residuals.append(residual)
        swaps.append(lax.ppermute(residual, "tok", swap))

    def own_terms(p, after):
        states = tie((mine, residuals[p], after))
        firsts.append(product(states[0], states[1], 0, 0))

    def other_terms(p, after):
        states = tie((other, swaps[p], after))
        terms = firsts[p] + product(states[0], states[1], 0, 0)
        all_terms.append(tie(terms).reshape(chips, own, width))

    def exchange(p, s):
        ups = [(2 * i + c, 2 * i + 2 + c) for i in range(s + 1) for c in range(2)]
        downs = [(tok - 1 - a, tok - 1 - b) for a, b in ups]
        send = (
            pick(all_terms[p], jnp.minimum(chips - 1 - s + chip, chips - 1)),
            pick(all_terms[p], jnp.maximum(s - (chips - 1) + chip, 0)),
        )
        if s:
            send = (send[0] + got[p][0], send[1] + got[p][1])
        send = tie((send, done[-2:-1]))[0]
        moved = lax.ppermute(send[0], "tok", ups), lax.ppermute(send[1], "tok", downs)
        got[p] = tie(moved)
        done.append(got[p])

    share = projector.shape[0] // PIECES
    student_parts = []

    def student_part(p, after):
        residual = jnp.concatenate(residuals, axis=1)
        held = tie((residual, after))[0]
        block = projector[p * share : (p + 1) * share]
        student_parts.append(product(held, block, 1, 1))

    steps = []
    for p in range(PIECES):
        steps += [(predict, p), (own_terms, p), (other_terms, p)]
    ahead, steps = steps[:6], steps[6:] + [(student_part, p) for p in range(PIECES)]
    after = row_scale
    for step, p in ahead:
        step(p, after)
    order = []
    for p in range(0, PIECES, 2):
        order += [(q, s) for s in range(chips - 1) for q in (p, p + 1)]
    for k, (p, s) in enumerate(order):
        exchange(p, s)
        if k >= 1 and steps:
            step, q = steps.pop(0)
            step(q, done[k - 1])
        if k == len(order) - 2:
            squares_of = [tie((r, done[k - 1]))[0] for r in residuals]
            error_sum = sum(jnp.sum(r * r) for r in squares_of)
            error_total = lax.psum(error_sum, ("tok", "feat"))
    student_terms = jnp.concatenate(student_parts, axis=1)
    student_grad = lax.psum_scatter(student_terms, "feat", scatter_dimension=1, tiled=True)
    loss_value = error_total / (token_count * cols * feat)
    totals = [pick(all_terms[p], chip) + got[p][0] + got[p][1] for p in range(PIECES)]

    proj_grad = jnp.concatenate(totals, axis=1) / token_count
    new_momentum = momentum_rate * momentum + proj_grad
    own_rows = lax.dynamic_slice_in_dim(projector, me * own, own, 0)
    new_projector = own_rows - step_rate * new_momentum
    return (new_projector, new_momentum, student_grad, loss_value)


def solution(mesh):
    in_specs = (P("tok", "feat"), P("tok", "feat"), P("feat"), P(None, "feat"), P("tok", "feat"))
    out_specs = (P("tok", "feat"), P("tok", "feat"), P("tok", "feat"), P())
    return jax.shard_map(
        on_device, mesh=mesh, in_specs=in_specs, out_specs=out_specs, check_vma=False
    )
```
